512 devices in a mesh: row: 16 (over y, x), col: 32 (over z, core).
Axes of the slice: x: 4, y: 4, z: 16, core: 2. Of those that a mesh axis runs over, the one named last changes fastest.
Arguments:
- tokens: bfloat16 [512, 8192], P('col', 'row'), may hold values from -6 to 6
- w_gate: bfloat16 [8192, 16384], P('row', 'col'), may hold values from -0.0625 to 0.0625
- w_up: bfloat16 [8192, 16384], P('row', 'col'), may hold values from -0.0625 to 0.0625
- w_down: bfloat16 [16384, 8192], P('col', 'row'), may hold values from -0.046875 to 0.046875
- upstream: bfloat16 [512, 8192], P('col', 'row'), may hold values from -3 to 3
Outputs:
- grad_tokens: bfloat16 [512, 8192], P('col', 'row')
- grad_gate: bfloat16 [8192, 16384], P('row', 'col')
- grad_up: bfloat16 [8192, 16384], P('row', 'col')
- grad_down: bfloat16 [16384, 8192], P('col', 'row')
The draws below stay inside these ranges and needn't reach their ends.
All inputs are finite; a program needn't handle non-finite values.
Results may differ from the reference program's by a relative error of at most 0.0049.
Values may be sent and summed in bfloat16 or wider, within the bound.
A program may use at most 64 MiB of HBM per device.

```python
import jax
import jax.numpy as jnp

D = 8192
FF = 16384
TOKENS = 512


def level_of(stream_key, extent, split, least, high):
    def one(dim, blocks):
        draws = jax.random.uniform(jax.random.fold_in(jax.random.fold_in(stream_key, 6), dim), (blocks,), jnp.float32, least / len(split), high / len(split))
        return jnp.repeat(jnp.exp(draws), extent[dim] // blocks).reshape((-1,) + (1,) * (len(extent) - dim - 1))

    factor_of = one(*split[0])
    for cut in split[1:]:
        factor_of = factor_of * one(*cut)
    return factor_of


def centred(rng, dims, scale, most, shards=(), held_as=jnp.bfloat16):
    drawn = scale * jax.random.normal(rng, dims, jnp.float32)
    if shards:
        drawn = drawn * level_of(rng, dims, shards, -0.22, 0.18)
    return jnp.clip(drawn, -most, most).astype(held_as)


def setup_inputs(seed: int = 0) -> dict:
    splits = jax.random.split(jax.random.key(seed), 6)
    tokens = centred(splits[0], (TOKENS, D), 1.0, 6.0, ((0, 32), (1, 16)))
    w_gate = centred(splits[1], (D, FF), D ** -0.5, 0.0625, ((0, 16), (1, 32)))
    w_up = centred(splits[2], (D, FF), D ** -0.5, 0.0625, ((0, 16), (1, 32)))
    w_down = centred(splits[3], (FF, D), FF ** -0.5, 0.046875, ((0, 32), (1, 16)))
    upstream = centred(splits[4], (TOKENS, D), 0.5, 3.0, ((0, 32), (1, 16)))
    return dict(tokens=tokens, w_gate=w_gate, w_up=w_up, w_down=w_down, upstream=upstream)


def reference(tokens, w_gate, w_up, w_down, upstream):
    gate_sum = jnp.dot(tokens, w_gate, preferred_element_type=jnp.float32)
    up_sum = jnp.dot(tokens, w_up, preferred_element_type=jnp.float32)
    slope_sum = jnp.dot(upstream, w_down.T, preferred_element_type=jnp.float32)
    logistic = 1.0 / (1.0 + jnp.exp(-gate_sum))
    activated = gate_sum * logistic
    hidden = (activated * up_sum).astype(jnp.bfloat16)
    hidden_grad_gate = (slope_sum * up_sum * logistic * (1.0 + gate_sum * (1.0 - logistic))).astype(jnp.bfloat16)
    hidden_grad_up = (slope_sum * activated).astype(jnp.bfloat16)
    grad_down = jnp.dot(hidden.T, upstream, preferred_element_type=jnp.float32).astype(jnp.bfloat16)
    grad_gate = jnp.dot(tokens.T, hidden_grad_gate, preferred_element_type=jnp.float32).astype(jnp.bfloat16)
    grad_up = jnp.dot(tokens.T, hidden_grad_up, preferred_element_type=jnp.float32).astype(jnp.bfloat16)
    grad_tokens = jnp.dot(hidden_grad_gate, w_gate.T, preferred_element_type=jnp.float32)
    grad_tokens = grad_tokens + jnp.dot(hidden_grad_up, w_up.T, preferred_element_type=jnp.float32)
    return (grad_tokens.astype(jnp.bfloat16), grad_gate, grad_up, grad_down)
```

```python
import jax
import jax.numpy as jnp
from jax import lax
from jax.experimental import pallas as pl
from jax.experimental.pallas import tpu as pltpu
from jax.sharding import PartitionSpec as P

MESH = pl.DeviceIdType.MESH
NX, NY, NZ = 4, 4, 16
CHUNKS = 4
ROWS = 128
B = 16
ORDER = [0, 1, -1, 2, -2, 3, -3, 4, -4, 5, -5, 6, -6, 7, -7, 8]
SLOT = {r: s for s, r in enumerate(ORDER)}
SLOT[-8] = SLOT[8]


def contract_last(left, right):
    return lax.dot_general(
        left, right, (((1,), (1,)), ((), ())), preferred_element_type=jnp.float32
    )


def contract_first(left, right):
    return lax.dot_general(
        left, right, (((0,), (0,)), ((), ())), preferred_element_type=jnp.float32
    )


def kernel(
    tokens_ref, wg_ref, wu_ref, wd_ref, upstream_ref,
    gt_ref, gg_ref, gu_ref, gd_ref,
    acts, weights, part, part16, got1, sum1, got2, hidden, inp, inp_got, inp16, inp_all, grads, gt_buf,
    in_sem, out_sem, a_send, a_recv, k_send, k_recv, b1_send, b1_recv, b2_send, b2_recv,
    c1_send, c1_recv, c2_send, c2_recv, e_send, e_recv, d_send, d_recv,
):
    row, col = lax.axis_index("row"), lax.axis_index("col")
    x, y = lax.rem(row, NX), lax.div(row, NX)
    z, core = lax.div(col, 2), lax.rem(col, 2)

    def along_x(d):
        return (y * NX + lax.rem(x + d, NX), col)

    def along_y(d):
        return (lax.rem(y + d, NY) * NX + x, col)

    def along_z(d):
        return (row, lax.rem(z + d % NZ, NZ) * 2 + core)

    sibling = (row, z * 2 + 1 - core)

    halves = ((along_x, x, along_y, y), (along_y, y, along_x, x))

    def put(src, dst, send, recv, peer):
        pltpu.make_async_remote_copy(
            src, dst, send, recv, device_id=peer, device_id_type=MESH
        ).start()

    def take(ref, sem):
        pltpu.make_async_copy(ref, ref, sem).wait()

    def shard(slot, c):
        return acts.at[:, pl.ds(pl.multiple_of(slot * 2 * B + c * B, B), B), :]

    mine = pl.ds(pl.multiple_of(core * B, B), B)
    loads = [
        pltpu.make_async_copy(tokens_ref, acts.at[0, mine, :], in_sem.at[0]),
        pltpu.make_async_copy(upstream_ref, acts.at[1, mine, :], in_sem.at[1]),
        pltpu.make_async_copy(wg_ref, weights.at[0], in_sem.at[2]),
        pltpu.make_async_copy(wu_ref, weights.at[1], in_sem.at[3]),
        pltpu.make_async_copy(wd_ref, weights.at[2], in_sem.at[4]),
    ]
    for load in loads:
        load.start()

    barrier = pltpu.get_barrier_semaphore()
    greet = [along_z(d) for d in (1, -1, 2, -2)] + [sibling]
    greet += [along_x(d) for d in (1, 2, 3)] + [along_y(d) for d in (1, 2, 3)]
    for peer in greet:
        pl.semaphore_signal(barrier, inc=1, device_id=peer, device_id_type=MESH)
    loads[0].wait()
    loads[1].wait()
    pl.semaphore_wait(barrier, len(greet))

    def gather_send(s):
        for sign in (1, -1):
            have = SLOT[-sign * 2 * s]
            for hop in (1, 2):
                rel = -sign * (2 * s + hop)
                if rel == 8:
                    continue
                put(
                    shard(have, core), shard(SLOT[rel], core), a_send.at[s], a_recv.at[s], along_z(sign * hop)
                )

    def gather_count(s):
        return 3 if s == 3 else 4

    def gather_take(s):
        n = gather_count(s)
        take(acts.at[:, 0 : n * B, :], a_recv.at[s])
        if s + 1 < 4:
            gather_send(s + 1)
        for rel in (2 * s + 1, -(2 * s + 1), 2 * s + 2, -(2 * s + 2)):
            if rel != -8:
                slot = SLOT[rel]
                put(shard(slot, core), shard(slot, core), k_send.at[s], k_recv.at[s], sibling)

    def project(c):
        rows = slice(c * ROWS, (c + 1) * ROWS)
        tok, ups = acts[0, rows, :], acts[1, rows, :]
        for i in range(3):
            if i < 2:
                p = jnp.dot(tok, weights[i], preferred_element_type=jnp.float32)
            else:
                p = contract_last(ups, weights[2])
            part[c, i] = p
            part16[c, i] = p.astype(jnp.bfloat16)
        for h, (first, at, _, _) in enumerate(halves):
            for d in (1, 2, 3):
                b = lax.rem(at + d, 4)
                block = pl.ds(pl.multiple_of(h * 64 + b * B, B), B)
                put(
                    part16.at[c, :, block, :], got1.at[c, h, d - 1], b1_send.at[c], b1_recv.at[c], first(d)
                )

    def add_first(c):
        take(got1.at[c], b1_recv.at[c])
        for h, (_, at, second, place) in enumerate(halves):
            block = pl.ds(pl.multiple_of(h * 64 + at * B, B), B)
            total = part[c, :, block, :]
            for d in range(3):
                total = total + got1[c, h, d].astype(jnp.float32)
            sum1[c, h] = total
            for d in (1, 2, 3):
                j = lax.rem(place + d, 4)
                cols = pl.ds(pl.multiple_of(j * 128, 128), 128)
                put(
                    sum1.at[c, h, :, :, cols], got2.at[c, h, d - 1], b2_send.at[c], b2_recv.at[c], second(d)
                )

    def own(c, h, at, place):
        rows = pl.ds(pl.multiple_of(c * ROWS + h * 64 + at * B, B), B)
        cols = pl.ds(pl.multiple_of(place * 128, 128), 128)
        return rows, cols

    def activate(c):
        take(got2.at[c], b2_recv.at[c])
        for h, (_, at, second, place) in enumerate(halves):
            rows, cols = own(c, h, at, place)
            total = sum1[c, h, :, :, cols]
            for d in range(3):
                total = total + got2[c, h, d]
            gate, up, slope = total[0], total[1], total[2]
            s = 1.0 / (1.0 + jnp.exp(-gate))
            activated = gate * s
            hidden[0, rows, cols] = (activated * up).astype(jnp.bfloat16)
            hidden[1, rows, cols] = (slope * up * s * (1.0 + gate * (1.0 - s))).astype(jnp.bfloat16)
            hidden[2, rows, cols] = (slope * activated).astype(jnp.bfloat16)
            block = hidden.at[:, rows, cols]
            for d in (1, 2, 3):
                put(block, block, c1_send.at[c], c1_recv.at[c], second(d))

    def spread(c):
        take(hidden.at[:, 0:96, 0:128], c1_recv.at[c])
        for h, (first, at, _, place) in enumerate(halves):
            rows, _ = own(c, h, at, place)
            block = hidden.at[:, rows, :]
            for d in (1, 2, 3):
                put(block, block, c2_send.at[c], c2_recv.at[c], first(d))

    def input_part(c):
        take(hidden.at[:, 0:96, :], c2_recv.at[c])
        rows = slice(c * ROWS, (c + 1) * ROWS)
        p = contract_last(hidden[1, rows, :], weights[0]) + contract_last(hidden[2, rows, :], weights[1])
        inp[c] = p.reshape(4, 2, B, 512)
        put(inp.at[c, :, 1 - core], inp_got.at[c], e_send.at[c], e_recv.at[c], sibling)

    def input_send(c):
        take(inp_got.at[c], e_recv.at[c])
        for i in range(4):
            slot = 4 * c + i
            total = inp[c, i, core] + inp_got[c, i]
            if slot == 0:
                inp_got[c, i] = total
            else:
                inp16[c, i] = total.astype(jnp.bfloat16)
                put(inp16.at[c, i], inp_all.at[slot - 1], d_send.at[0], d_recv.at[0], along_z(ORDER[slot]))

    def weight_grads():
        stores = []
        pairs = ((acts, 0, hidden, 1, gg_ref), (acts, 0, hidden, 2, gu_ref), (hidden, 0, acts, 1, gd_ref))
        for i, (left, li, right, ri, out) in enumerate(pairs):
            grads[i] = contract_first(left[li], right[ri]).astype(jnp.bfloat16)
            stores.append(pltpu.make_async_copy(grads.at[i], out, out_sem.at[i]))
            stores[-1].start()
        return stores

    def ready(c):
        if c == 0:
            shard0 = shard(0, core)
            put(shard0, shard0, k_send.at[4], k_recv.at[4], sibling)
            gather_send(0)
            gather_take(0)
            take(acts.at[:, 0:B, :], k_recv.at[4])
        n = gather_count(c)
        take(acts.at[:, 0 : n * B, :], k_recv.at[c])

    ready(0)
    for load in loads[2:]:
        load.wait()
    project(0)
    gather_take(1)
    ready(1)
    project(1)
    add_first(0)
    gather_take(2)
    ready(2)
    project(2)
    activate(0)
    add_first(1)
    gather_take(3)
    ready(3)
    project(3)
    spread(0)
    activate(1)
    add_first(2)
    input_part(0)
    spread(1)
    activate(2)
    add_first(3)
    input_send(0)
    input_part(1)
    spread(2)
    activate(3)
    input_send(1)
    input_part(2)
    spread(3)
    input_send(2)
    input_part(3)
    input_send(3)
    stores = weight_grads()

    take(inp_all, d_recv.at[0])
    total = inp_got[0, 0]
    for i in range(15):
        total = total + inp_all[i].astype(jnp.float32)
    gt_buf[...] = total.astype(jnp.bfloat16)
    stores.append(pltpu.make_async_copy(gt_buf, gt_ref, out_sem.at[3]))
    stores[-1].start()

    for s in range(4):
        n = gather_count(s)
        take(acts.at[:, 0 : n * B, :], a_send.at[s])
        take(acts.at[:, 0 : n * B, :], k_send.at[s])
    take(acts.at[:, 0:B, :], k_send.at[4])
    for c in range(CHUNKS):
        take(got1.at[c], b1_send.at[c])
        take(got2.at[c], b2_send.at[c])
        take(hidden.at[:, 0:96, 0:128], c1_send.at[c])
        take(hidden.at[:, 0:96, :], c2_send.at[c])
        take(inp_got.at[c], e_send.at[c])
    take(inp_all, d_send.at[0])
    for store in stores:
        store.wait()


def body(tokens, w_gate, w_up, w_down, upstream):
    bf16, f32 = jnp.bfloat16, jnp.float32
    sem = pltpu.SemaphoreType.DMA
    out = lambda *shape: jax.ShapeDtypeStruct(shape, bf16)
    return pl.pallas_call(
        kernel,
        name="mlp",
        out_shape=(out(16, 512), out(512, 512), out(512, 512), out(512, 512)),
        in_specs=[pl.BlockSpec(memory_space=pltpu.HBM)] * 5,
        out_specs=(pl.BlockSpec(memory_space=pltpu.HBM),) * 4,
        scratch_shapes=[
            pltpu.VMEM((2, 512, 512), bf16),
            pltpu.VMEM((3, 512, 512), bf16),
            pltpu.VMEM((CHUNKS, 3, ROWS, 512), f32),
            pltpu.VMEM((CHUNKS, 3, ROWS, 512), bf16),
            pltpu.VMEM((CHUNKS, 2, 3, 3, B, 512), bf16),
            pltpu.VMEM((CHUNKS, 2, 3, B, 512), f32),
            pltpu.VMEM((CHUNKS, 2, 3, 3, B, 128), f32),
            pltpu.VMEM((3, 512, 512), bf16),
            pltpu.VMEM((CHUNKS, 4, 2, B, 512), f32),
            pltpu.VMEM((CHUNKS, 4, B, 512), f32),
            pltpu.VMEM((CHUNKS, 4, B, 512), bf16),
            pltpu.VMEM((15, B, 512), bf16),
            pltpu.VMEM((3, 512, 512), bf16),
            pltpu.VMEM((B, 512), bf16),
            sem((5,)), sem((4,)),
            sem((4,)), sem((4,)), sem((5,)), sem((5,)),
            sem((4,)), sem((4,)), sem((4,)), sem((4,)),
            sem((4,)), sem((4,)), sem((4,)), sem((4,)),
            sem((4,)), sem((4,)), sem((1,)), sem((1,)),
        ],
        compiler_params=pltpu.CompilerParams(
            collective_id=0, has_side_effects=True, vmem_limit_bytes=60 << 20
        ),
        cost_estimate=pl.CostEstimate(flops=2 << 30, bytes_accessed=4 << 20, transcendentals=0),
    )(tokens, w_gate, w_up, w_down, upstream)


def solution(mesh):
    return jax.shard_map(
        body,
        mesh=mesh,
        in_specs=(P("col", "row"), P("row", "col"), P("row", "col"), P("col", "row"), P("col", "row")),
        out_specs=(P("col", "row"), P("row", "col"), P("row", "col"), P("col", "row")),
        check_vma=False,
    )
```

```python
import jax
import jax.numpy as jnp
from jax import lax
from jax.experimental import pallas as pl
from jax.experimental.pallas import tpu as pltpu
from jax.sharding import PartitionSpec as P

MESH = pl.DeviceIdType.MESH
NX, NY, NZ = 4, 4, 16
CHUNKS = 4
ROWS = 128
B = 16
ORDER = [0, 1, -1, 2, -2, 3, -3, 4, -4, 5, -5, 6, -6, 7, -7, 8]
SLOT = {r: s for s, r in enumerate(ORDER)}
SLOT[-8] = SLOT[8]
REACH = (3, 3, 2)
BASE = [sum(REACH[:s]) for s in range(len(REACH) + 1)]
STAGES = len(REACH)

SCHEDULE = (
    ("relay", 0),
    ("nearer", 0),
    ("project", 0),
    ("relay", 1),
    ("nearer", 1),
    ("project", 2),
    ("project", 1),
    ("relay", 2),
    ("nearer", 2),
    ("add", 2),
    ("project", 3),
    ("activate", 2),
    ("add", 1),
    ("add", 3),
    ("spread", 2),
    ("activate", 3),
    ("add", 0),
    ("activate", 1),
    ("product", 2),
    ("spread", 3),
    ("send", 2),
    ("activate", 0),
    ("product", 3),
    ("spread", 1),
    ("spread", 0),
    ("send", 3),
    ("product", 1),
    ("send", 1),
    ("product", 0),
    ("send", 0),
)


def contract_last(left, right):
    return lax.dot_general(
        left, right, (((1,), (1,)), ((), ())), preferred_element_type=jnp.float32
    )


def contract_first(left, right):
    return lax.dot_general(
        left, right, (((0,), (0,)), ((), ())), preferred_element_type=jnp.float32
    )


def kernel(
    tokens_ref, wg_ref, wu_ref, wd_ref, upstream_ref,
    gt_ref, gg_ref, gu_ref, gd_ref,
    acts, weights, part, part16, got1, sum1, got2, hidden, inp, inp_got, inp16, inp_all,
    in_sem, a_send, a_recv, k_send, k_recv, b1_send, b1_recv, b2_send, b2_recv,
    c1_send, c1_recv, c2_send, c2_recv, e_send, e_recv, d_send, d_recv,
):
    row, col = lax.axis_index("row"), lax.axis_index("col")
    x, y = lax.rem(row, NX), lax.div(row, NX)
    z, core = lax.div(col, 2), lax.rem(col, 2)

    def along_x(d):
        return (y * NX + lax.rem(x + d, NX), col)

    def along_y(d):
        return (lax.rem(y + d, NY) * NX + x, col)

    def along_z(d):
        return (row, lax.rem(z + d % NZ, NZ) * 2 + core)

    sibling = (row, z * 2 + 1 - core)

    halves = ((along_x, x, along_y, y), (along_y, y, along_x, x))

    def put(src, dst, send, recv, peer):
        pltpu.make_async_remote_copy(
            src, dst, send, recv, device_id=peer, device_id_type=MESH
        ).start()

    def take(ref, sem):
        pltpu.make_async_copy(ref, ref, sem).wait()

    def shard(slot, c):
        return acts.at[:, pl.ds(pl.multiple_of(slot * 2 * B + c * B, B), B), :]

    mine = pl.ds(pl.multiple_of(core * B, B), B)
    loads = [
        pltpu.make_async_copy(tokens_ref, acts.at[0, mine, :], in_sem.at[0]),
        pltpu.make_async_copy(upstream_ref, acts.at[1, mine, :], in_sem.at[1]),
        pltpu.make_async_copy(wg_ref, weights.at[0], in_sem.at[2]),
        pltpu.make_async_copy(wu_ref, weights.at[1], in_sem.at[3]),
        pltpu.make_async_copy(wd_ref, weights.at[2], in_sem.at[4]),
    ]
    for load in loads:
        load.start()

    barrier = pltpu.get_barrier_semaphore()
    greet = [along_z(sign * d) for d in range(1, max(REACH) + 1) for sign in (1, -1)] + [sibling]
    greet += [along_x(d) for d in (1, 2, 3)] + [along_y(d) for d in (1, 2, 3)]
    for peer in greet:
        pl.semaphore_signal(barrier, inc=1, device_id=peer, device_id_type=MESH)
    loads[0].wait()
    loads[1].wait()
    pl.semaphore_wait(barrier, len(greet))

    def far(s):
        return [r for r in (BASE[s + 1], -BASE[s + 1]) if r != -8]

    def near(s):
        return [sign * d for d in range(BASE[s] + 1, BASE[s + 1]) for sign in (1, -1)]

    def gather_send(s):
        for hop in range(REACH[s], 0, -1):
            for sign in (1, -1):
                have, rel = -sign * BASE[s], -sign * (BASE[s] + hop)
                if rel == 8:
                    rel = -8 if sign > 0 else 8
                if rel == 8:
                    continue
                relay = 2 * s + int(hop == REACH[s])
                put(
                    shard(SLOT[have], core), shard(SLOT[rel], core),
                    a_send.at[relay], a_recv.at[relay], along_z(sign * hop),
                )

    def to_sibling(rels, sem):
        for rel in rels:
            put(shard(SLOT[rel], core), shard(SLOT[rel], core), k_send.at[sem], k_recv.at[sem], sibling)

    def few(n):
        return acts.at[:, 0 : n * B, :]

    groups = [f(s) for s in range(STAGES) for f in (near, far)]

    def relay(s):
        take(few(len(far(s))), a_recv.at[2 * s + 1])
        if s + 1 < STAGES:
            gather_send(s + 1)
        to_sibling(far(s), 2 * s + 1)

    def nearer(s):
        if near(s):
            take(few(len(near(s))), a_recv.at[2 * s])
            to_sibling(near(s), 2 * s)

    here = []

    def project(c):
        for rel in ORDER[4 * c : 4 * c + 4]:
            group = next((g for g, rels in enumerate(groups) if rel in rels), 2 * STAGES)
            if group not in here:
                here.append(group)
                take(few(len(groups[group]) if rel else 1), k_recv.at[group])
        rows = slice(c * ROWS, (c + 1) * ROWS)
        tok, ups = acts[0, rows, :], acts[1, rows, :]
        for i in range(3):
            if i < 2:
                p = jnp.dot(tok, weights[i], preferred_element_type=jnp.float32)
            else:
                p = contract_last(ups, weights[2])
            part[c, i] = p
            part16[c, i] = p.astype(jnp.bfloat16)
        for h, (first, at, _, _) in enumerate(halves):
            for d in (1, 2, 3):
                b = lax.rem(at + d, 4)
                block = pl.ds(pl.multiple_of(h * 64 + b * B, B), B)
                put(
                    part16.at[c, :, block, :], got1.at[c, h, d - 1], b1_send.at[c], b1_recv.at[c], first(d)
                )

    def add_first(c):
        take(got1.at[c], b1_recv.at[c])
        for h, (_, at, second, place) in enumerate(halves):
            block = pl.ds(pl.multiple_of(h * 64 + at * B, B), B)
            total = part[c, :, block, :]
            for d in range(3):
                total = total + got1[c, h, d].astype(jnp.float32)
            sum1[c, h] = total
            for d in (1, 2, 3):
                j = lax.rem(place + d, 4)
                cols = pl.ds(pl.multiple_of(j * 128, 128), 128)
                put(
                    sum1.at[c, h, :, :, cols], got2.at[c, h, d - 1], b2_send.at[c], b2_recv.at[c], second(d)
                )

    def own(c, h, at, place):
        rows = pl.ds(pl.multiple_of(c * ROWS + h * 64 + at * B, B), B)
        cols = pl.ds(pl.multiple_of(place * 128, 128), 128)
        return rows, cols

    def activate(c):
        take(got2.at[c], b2_recv.at[c])
        for h, (_, at, second, place) in enumerate(halves):
            rows, cols = own(c, h, at, place)
            total = sum1[c, h, :, :, cols]
            for d in range(3):
                total = total + got2[c, h, d]
            gate, up, slope = total[0], total[1], total[2]
            s = 1.0 / (1.0 + jnp.exp(-gate))
            activated = gate * s
            hidden[0, rows, cols] = (activated * up).astype(jnp.bfloat16)
            hidden[1, rows, cols] = (slope * up * s * (1.0 + gate * (1.0 - s))).astype(jnp.bfloat16)
            hidden[2, rows, cols] = (slope * activated).astype(jnp.bfloat16)
            block = hidden.at[:, rows, cols]
            for d in (1, 2, 3):
                put(block, block, c1_send.at[c], c1_recv.at[c], second(d))

    def spread(c):
        take(hidden.at[:, 0:96, 0:128], c1_recv.at[c])
        for h, (first, at, _, place) in enumerate(halves):
            rows, _ = own(c, h, at, place)
            block = hidden.at[:, rows, :]
            for d in (1, 2, 3):
                put(block, block, c2_send.at[c], c2_recv.at[c], first(d))

    def input_part(c):
        take(hidden.at[:, 0:96, :], c2_recv.at[c])
        rows = slice(c * ROWS, (c + 1) * ROWS)
        p = contract_last(hidden[1, rows, :], weights[0]) + contract_last(hidden[2, rows, :], weights[1])
        inp[c] = p.reshape(4, 2, B, 512)
        put(inp.at[c, :, 1 - core], inp_got.at[c], e_send.at[c], e_recv.at[c], sibling)

    def input_send(c):
        take(inp_got.at[c], e_recv.at[c])
        for i in range(4):
            slot = 4 * c + i
            total = inp[c, i, core] + inp_got[c, i]
            if slot == 0:
                inp_got[c, i] = total
            else:
                inp16[c, i] = total.astype(jnp.bfloat16)
                put(inp16.at[c, i], inp_all.at[slot - 1], d_send.at[0], d_recv.at[0], along_z(ORDER[slot]))

    def weight_grads():
        pairs = ((acts, 0, hidden, 1, gg_ref), (acts, 0, hidden, 2, gu_ref), (hidden, 0, acts, 1, gd_ref))
        for left, li, right, ri, out in pairs:
            out[...] = contract_first(left[li], right[ri]).astype(jnp.bfloat16)

    gather_send(0)
    to_sibling((0,), 2 * STAGES)
    loaded = False
    tasks = dict(
        relay=relay, nearer=nearer, project=project, add=add_first, activate=activate, spread=spread,
        product=input_part, send=input_send,
    )
    for name, c in SCHEDULE:
        if name == "project" and not loaded:
            for load in loads[2:]:
                load.wait()
            loaded = True
        tasks[name](c)
    weight_grads()

    take(inp_all, d_recv.at[0])
    total = inp_got[0, 0]
    for i in range(15):
        total = total + inp_all[i].astype(jnp.float32)
    gt_ref[...] = total.astype(jnp.bfloat16)

    for group, rels in enumerate(groups):
        if rels:
            take(few(len(rels)), a_send.at[group])
            take(few(len(rels)), k_send.at[group])
    take(few(1), k_send.at[2 * STAGES])
    for c in range(CHUNKS):
        take(got1.at[c], b1_send.at[c])
        take(got2.at[c], b2_send.at[c])
        take(hidden.at[:, 0:96, 0:128], c1_send.at[c])
        take(hidden.at[:, 0:96, :], c2_send.at[c])
        take(inp_got.at[c], e_send.at[c])
    take(inp_all, d_send.at[0])


def write_out(*refs):
    sems = refs[8]
    copies = [pltpu.make_async_copy(refs[i], refs[4 + i], sems.at[i]) for i in range(4)]
    for copy in copies:
        copy.start()
    for copy in copies:
        copy.wait()


def body(tokens, w_gate, w_up, w_down, upstream):
    bf16, f32 = jnp.bfloat16, jnp.float32
    sem = pltpu.SemaphoreType.DMA
    shapes = ((16, 512), (512, 512), (512, 512), (512, 512))
    results = pl.pallas_call(
        kernel,
        name="mlp",
        out_shape=tuple(pltpu.VMEM(shape, bf16) for shape in shapes),
        in_specs=[pl.BlockSpec(memory_space=pltpu.HBM)] * 5,
        out_specs=(pl.BlockSpec(memory_space=pltpu.VMEM),) * 4,
        scratch_shapes=[
            pltpu.VMEM((2, 512, 512), bf16),
            pltpu.VMEM((3, 512, 512), bf16),
            pltpu.VMEM((CHUNKS, 3, ROWS, 512), f32),
            pltpu.VMEM((CHUNKS, 3, ROWS, 512), bf16),
            pltpu.VMEM((CHUNKS, 2, 3, 3, B, 512), bf16),
            pltpu.VMEM((CHUNKS, 2, 3, B, 512), f32),
            pltpu.VMEM((CHUNKS, 2, 3, 3, B, 128), f32),
            pltpu.VMEM((3, 512, 512), bf16),
            pltpu.VMEM((CHUNKS, 4, 2, B, 512), f32),
            pltpu.VMEM((CHUNKS, 4, B, 512), f32),
            pltpu.VMEM((CHUNKS, 4, B, 512), bf16),
            pltpu.VMEM((15, B, 512), bf16),
            sem((5,)),
            sem((2 * STAGES,)), sem((2 * STAGES,)), sem((2 * STAGES + 1,)), sem((2 * STAGES + 1,)),
            sem((4,)), sem((4,)), sem((4,)), sem((4,)),
            sem((4,)), sem((4,)), sem((4,)), sem((4,)),
            sem((4,)), sem((4,)), sem((1,)), sem((1,)),
        ],
        compiler_params=pltpu.CompilerParams(
            collective_id=0, has_side_effects=True, vmem_limit_bytes=60 << 20
        ),
        cost_estimate=pl.CostEstimate(flops=2 << 30, bytes_accessed=4 << 20, transcendentals=0),
    )(tokens, w_gate, w_up, w_down, upstream)
    results = [pltpu.with_memory_space_constraint(r, pltpu.VMEM) for r in results]
    return pl.pallas_call(
        write_out,
        name="write_out",
        out_shape=tuple(jax.ShapeDtypeStruct(shape, bf16) for shape in shapes),
        in_specs=[pl.BlockSpec(memory_space=pltpu.VMEM)] * 4,
        out_specs=(pl.BlockSpec(memory_space=pltpu.HBM),) * 4,
        scratch_shapes=[sem((4,))],
    )(*results)


def solution(mesh):
    return jax.shard_map(
        body,
        mesh=mesh,
        in_specs=(P("col", "row"), P("row", "col"), P("row", "col"), P("col", "row"), P("col", "row")),
        out_specs=(P("col", "row"), P("row", "col"), P("row", "col"), P("col", "row")),
        check_vma=False,
    )
```

```python
import jax
import jax.numpy as jnp
from jax import lax
from jax.experimental import pallas as pl
from jax.experimental.pallas import tpu as pltpu
from jax.sharding import PartitionSpec as P

MESH = pl.DeviceIdType.MESH
NX, NY, NZ = 4, 4, 16
CHUNKS = 4
ROWS = 128
B = 16
ORDER = [0, 1, -1, 2, 3, -3, 4, -4, 5, -5, 6, -6, -2, 7, -7, 8]
SLOT = {r: s for s, r in enumerate(ORDER)}
SLOT[-8] = SLOT[8]
REACH = (3, 3, 2)
BASE = [sum(REACH[:s]) for s in range(len(REACH) + 1)]
STAGES = len(REACH)

LAST = (0, 2, 1, 3)
SCHEDULE = (
    ("relay", 0),
    ("nearer", 0),
    ("project", 0),
    ("relay", 1),
    ("nearer", 1),
    ("project", 2),
    ("relay", 2),
    ("nearer", 2),
    ("add", 0),
    ("project", 3),
    ("add", 2),
    ("project", 1),
    ("add", 3),
    ("activate", 2),
    ("activate", 0),
    ("add", 1),
    ("activate", 3),
    ("spread", 2),
    ("spread", 3),
    ("activate", 1),
    ("product", 2),
    ("send", 2),
    ("spread", 0),
    ("product", 3),
    ("send", 3),
    ("spread", 1),
    ("product", 0),
    ("send", 0),
    ("product", 1),
    ("send", 1),
)


def contract_last(left, right):
    return lax.dot_general(
        left, right, (((1,), (1,)), ((), ())), preferred_element_type=jnp.float32
    )


def contract_first(left, right):
    return lax.dot_general(
        left, right, (((0,), (0,)), ((), ())), preferred_element_type=jnp.float32
    )


def kernel(
    tokens_ref, wg_ref, wu_ref, wd_ref, upstream_ref,
    gt_ref, gg_ref, gu_ref, gd_ref,
    acts, weights, part, part16, got1, sum1, got2, hidden, inp, inp_got, inp16, inp_all,
    in_sem, a_send, a_recv, k_send, k_recv, b1_send, b1_recv, b2_send, b2_recv,
    c1_send, c1_recv, c2_send, c2_recv, e_send, e_recv, d_send, d_recv,
):
    row, col = lax.axis_index("row"), lax.axis_index("col")
    x, y = lax.rem(row, NX), lax.div(row, NX)
    z, core = lax.div(col, 2), lax.rem(col, 2)

    def along_x(d):
        return (y * NX + lax.rem(x + d, NX), col)

    def along_y(d):
        return (lax.rem(y + d, NY) * NX + x, col)

    def along_z(d):
        return (row, lax.rem(z + d % NZ, NZ) * 2 + core)

    sibling = (row, z * 2 + 1 - core)

    halves = ((along_x, x, along_y, y), (along_y, y, along_x, x))

    def put(src, dst, send, recv, peer):
        pltpu.make_async_remote_copy(
            src, dst, send, recv, device_id=peer, device_id_type=MESH
        ).start()

    def take(ref, sem):
        pltpu.make_async_copy(ref, ref, sem).wait()

    def shard(slot, c):
        return acts.at[:, pl.ds(pl.multiple_of(slot * 2 * B + c * B, B), B), :]

    mine = pl.ds(pl.multiple_of(core * B, B), B)
    loads = [
        pltpu.make_async_copy(tokens_ref, acts.at[0, mine, :], in_sem.at[0]),
        pltpu.make_async_copy(upstream_ref, acts.at[1, mine, :], in_sem.at[1]),
        pltpu.make_async_copy(wg_ref, weights.at[0], in_sem.at[2]),
        pltpu.make_async_copy(wu_ref, weights.at[1], in_sem.at[3]),
        pltpu.make_async_copy(wd_ref, weights.at[2], in_sem.at[4]),
    ]
    for load in loads:
        load.start()

    barrier = pltpu.get_barrier_semaphore()
    greet = [along_z(sign * d) for d in range(1, max(REACH) + 1) for sign in (1, -1)] + [sibling]
    greet += [along_x(d) for d in (1, 2, 3)] + [along_y(d) for d in (1, 2, 3)]
    for peer in greet:
        pl.semaphore_signal(barrier, inc=1, device_id=peer, device_id_type=MESH)
    loads[0].wait()
    loads[1].wait()
    pl.semaphore_wait(barrier, len(greet))

    def far(s):
        return [r for r in (BASE[s + 1], -BASE[s + 1]) if r != -8]

    def near(s):
        return [sign * d for d in range(BASE[s] + 1, BASE[s + 1]) for sign in (1, -1)]

    def gather_send(s):
        for hop in range(REACH[s], 0, -1):
            for sign in (1, -1):
                have, rel = -sign * BASE[s], -sign * (BASE[s] + hop)
                if rel == 8:
                    rel = -8 if sign > 0 else 8
                if rel == 8:
                    continue
                relay = 2 * s + int(hop == REACH[s])
                put(
                    shard(SLOT[have], core), shard(SLOT[rel], core),
                    a_send.at[relay], a_recv.at[relay], along_z(sign * hop),
                )

    def to_sibling(rels, sem):
        for rel in rels:
            put(shard(SLOT[rel], core), shard(SLOT[rel], core), k_send.at[sem], k_recv.at[sem], sibling)

    def few(n):
        return acts.at[:, 0 : n * B, :]

    groups = [f(s) for s in range(STAGES) for f in (near, far)]

    def relay(s):
        take(few(len(far(s))), a_recv.at[2 * s + 1])
        if s + 1 < STAGES:
            gather_send(s + 1)
        to_sibling(far(s), 2 * s + 1)

    def nearer(s):
        if near(s):
            take(few(len(near(s))), a_recv.at[2 * s])
            to_sibling(near(s), 2 * s)

    here = []

    def project(c):
        for rel in ORDER[4 * c : 4 * c + 4]:
            group = next((g for g, rels in enumerate(groups) if rel in rels), 2 * STAGES)
            if group not in here:
                here.append(group)
                take(few(len(groups[group]) if rel else 1), k_recv.at[group])
        rows = slice(c * ROWS, (c + 1) * ROWS)
        tok, ups = acts[0, rows, :], acts[1, rows, :]
        for i in range(3):
            if i < 2:
                p = jnp.dot(tok, weights[i], preferred_element_type=jnp.float32)
            else:
                p = contract_last(ups, weights[2])
            part[c, i] = p
            part16[c, i] = p.astype(jnp.bfloat16)
        for d in (2, 1, 3):
            for h, (first, at, _, _) in enumerate(halves):
                b = lax.rem(at + d, 4)
                block = pl.ds(pl.multiple_of(h * 64 + b * B, B), B)
                put(
                    part16.at[c, :, block, :], got1.at[c, h, d - 1], b1_send.at[c], b1_recv.at[c], first(d)
                )

    def add_first(c):
        take(got1.at[c], b1_recv.at[c])
        for h, (_, at, second, place) in enumerate(halves):
            block = pl.ds(pl.multiple_of(h * 64 + at * B, B), B)
            total = part[c, :, block, :]
            for d in range(3):
                total = total + got1[c, h, d].astype(jnp.float32)
            sum1[c, h] = total
        for d in (2, 1, 3):
            for h, (_, _, second, place) in enumerate(halves):
                j = lax.rem(place + d, 4)
                cols = pl.ds(pl.multiple_of(j * 128, 128), 128)
                put(
                    sum1.at[c, h, :, :, cols], got2.at[c, h, d - 1], b2_send.at[c], b2_recv.at[c], second(d)
                )

    def own(c, h, at, place):
        rows = pl.ds(pl.multiple_of(c * ROWS + h * 64 + at * B, B), B)
        cols = pl.ds(pl.multiple_of(place * 128, 128), 128)
        return rows, cols

    def activate(c):
        take(got2.at[c], b2_recv.at[c])
        for h, (_, at, second, place) in enumerate(halves):
            rows, cols = own(c, h, at, place)
            total = sum1[c, h, :, :, cols]
            for d in range(3):
                total = total + got2[c, h, d]
            gate, up, slope = total[0], total[1], total[2]
            s = 1.0 / (1.0 + jnp.exp(-gate))
            activated = gate * s
            hidden[0, rows, cols] = (activated * up).astype(jnp.bfloat16)
            hidden[1, rows, cols] = (slope * up * s * (1.0 + gate * (1.0 - s))).astype(jnp.bfloat16)
            hidden[2, rows, cols] = (slope * activated).astype(jnp.bfloat16)
        for d in (2, 1, 3):
            for h, (_, at, second, place) in enumerate(halves):
                rows, cols = own(c, h, at, place)
                block = hidden.at[:, rows, cols]
                put(block, block, c1_send.at[c], c1_recv.at[c], second(d))

    def spread(c):
        take(hidden.at[:, 0:96, 0:128], c1_recv.at[c])
        for d in (2, 1, 3):
            for h, (first, at, _, place) in enumerate(halves):
                rows, _ = own(c, h, at, place)
                block = hidden.at[:, rows, :]
                put(block, block, c2_send.at[c], c2_recv.at[c], first(d))

    def input_part(c):
        take(hidden.at[:, 0:96, :], c2_recv.at[c])
        rows = slice(c * ROWS, (c + 1) * ROWS)
        p = contract_last(hidden[1, rows, :], weights[0]) + contract_last(hidden[2, rows, :], weights[1])
        inp[c] = p.reshape(4, 2, B, 512)
        put(inp.at[c, :, 1 - core], inp_got.at[c], e_send.at[c], e_recv.at[c], sibling)

    def input_send(c):
        take(inp_got.at[c], e_recv.at[c])
        for i in reversed(range(4)):
            slot = 4 * c + i
            total = inp[c, i, core] + inp_got[c, i]
            if slot == 0:
                inp_got[c, i] = total
            else:
                inp16[c, i] = total.astype(jnp.bfloat16)
                put(inp16.at[c, i], inp_all.at[slot - 1], d_send.at[0], d_recv.at[c], along_z(ORDER[slot]))

    def weight_grads():
        pairs = ((acts, 0, hidden, 1, gg_ref), (acts, 0, hidden, 2, gu_ref), (hidden, 0, acts, 1, gd_ref))
        for left, li, right, ri, out in pairs:
            out[...] = contract_first(left[li], right[ri]).astype(jnp.bfloat16)

    gather_send(0)
    to_sibling((0,), 2 * STAGES)
    loaded = False
    tasks = dict(
        relay=relay, nearer=nearer, project=project, add=add_first, activate=activate, spread=spread,
        product=input_part, send=input_send,
    )
    for name, c in SCHEDULE:
        if name == "project" and not loaded:
            for load in loads[2:]:
                load.wait()
            loaded = True
        tasks[name](c)
    weight_grads()

    for group, rels in enumerate(groups):
        if rels:
            take(few(len(rels)), a_send.at[group])
            take(few(len(rels)), k_send.at[group])
    take(few(1), k_send.at[2 * STAGES])
    for c in range(CHUNKS):
        take(got1.at[c], b1_send.at[c])
        take(got2.at[c], b2_send.at[c])
        take(hidden.at[:, 0:96, 0:128], c1_send.at[c])
        take(hidden.at[:, 0:96, :], c2_send.at[c])
        take(inp_got.at[c], e_send.at[c])

    total = inp_got[0, 0]
    for c in LAST:
        slots = range(max(4 * c, 1), 4 * c + 4)
        take(inp_all.at[slots[0] - 1 : slots[-1]], d_recv.at[c])
        for slot in slots:
            total = total + inp_all[slot - 1].astype(jnp.float32)
    gt_ref[...] = total.astype(jnp.bfloat16)
    take(inp_all, d_send.at[0])


def write_out(*refs):
    sems = refs[8]
    copies = [pltpu.make_async_copy(refs[i], refs[4 + i], sems.at[i]) for i in range(4)]
    for copy in copies:
        copy.start()
    for copy in copies:
        copy.wait()


def body(tokens, w_gate, w_up, w_down, upstream):
    bf16, f32 = jnp.bfloat16, jnp.float32
    sem = pltpu.SemaphoreType.DMA
    shapes = ((16, 512), (512, 512), (512, 512), (512, 512))
    results = pl.pallas_call(
        kernel,
        name="mlp",
        out_shape=tuple(pltpu.VMEM(shape, bf16) for shape in shapes),
        in_specs=[pl.BlockSpec(memory_space=pltpu.HBM)] * 5,
        out_specs=(pl.BlockSpec(memory_space=pltpu.VMEM),) * 4,
        scratch_shapes=[
            pltpu.VMEM((2, 512, 512), bf16),
            pltpu.VMEM((3, 512, 512), bf16),
            pltpu.VMEM((CHUNKS, 3, ROWS, 512), f32),
            pltpu.VMEM((CHUNKS, 3, ROWS, 512), bf16),
            pltpu.VMEM((CHUNKS, 2, 3, 3, B, 512), bf16),
            pltpu.VMEM((CHUNKS, 2, 3, B, 512), f32),
            pltpu.VMEM((CHUNKS, 2, 3, 3, B, 128), f32),
            pltpu.VMEM((3, 512, 512), bf16),
            pltpu.VMEM((CHUNKS, 4, 2, B, 512), f32),
            pltpu.VMEM((CHUNKS, 4, B, 512), f32),
            pltpu.VMEM((CHUNKS, 4, B, 512), bf16),
            pltpu.VMEM((15, B, 512), bf16),
            sem((5,)),
            sem((2 * STAGES,)), sem((2 * STAGES,)), sem((2 * STAGES + 1,)), sem((2 * STAGES + 1,)),
            sem((4,)), sem((4,)), sem((4,)), sem((4,)),
            sem((4,)), sem((4,)), sem((4,)), sem((4,)),
            sem((4,)), sem((4,)), sem((1,)), sem((4,)),
        ],
        compiler_params=pltpu.CompilerParams(
            collective_id=0, has_side_effects=True, vmem_limit_bytes=60 << 20
        ),
        cost_estimate=pl.CostEstimate(flops=2 << 30, bytes_accessed=4 << 20, transcendentals=0),
    )(tokens, w_gate, w_up, w_down, upstream)
    results = [pltpu.with_memory_space_constraint(r, pltpu.VMEM) for r in results]
    return pl.pallas_call(
        write_out,
        name="write_out",
        out_shape=tuple(jax.ShapeDtypeStruct(shape, bf16) for shape in shapes),
        in_specs=[pl.BlockSpec(memory_space=pltpu.VMEM)] * 4,
        out_specs=(pl.BlockSpec(memory_space=pltpu.HBM),) * 4,
        scratch_shapes=[sem((4,))],
    )(*results)


def solution(mesh):
    return jax.shard_map(
        body,
        mesh=mesh,
        in_specs=(P("col", "row"), P("row", "col"), P("row", "col"), P("col", "row"), P("col", "row")),
        out_specs=(P("col", "row"), P("row", "col"), P("row", "col"), P("col", "row")),
        check_vma=False,
    )
```

```python
import jax
import jax.numpy as jnp
from jax import lax
from jax.experimental import pallas as pl
from jax.experimental.pallas import tpu as pltpu
from jax.sharding import PartitionSpec as P

MESH = pl.DeviceIdType.MESH
NX, NY, NZ = 4, 4, 16
CHUNKS = 4
ROWS = 128
B = 16
ORDER = [0, 1, -1, 2, 3, -3, 4, -4, 5, -5, 6, -6, -2, 7, -7, 8]
SLOT = {r: s for s, r in enumerate(ORDER)}
SLOT[-8] = SLOT[8]
REACH = (3, 3, 2)
BASE = [sum(REACH[:s]) for s in range(len(REACH) + 1)]
STAGES = len(REACH)

LAST = (0, 2, 1, 3)
SCHEDULE = (
    ("relay", 0),
    ("nearer", 0),
    ("project", 0),
    ("relay", 1),
    ("nearer", 1),
    ("project", 2),
    ("relay", 2),
    ("nearer", 2),
    ("add", 0),
    ("project", 3),
    ("add", 2),
    ("project", 1),
    ("add", 3),
    ("activate", 2),
    ("activate", 0),
    ("add", 1),
    ("activate", 3),
    ("spread", 2),
    ("spread", 3),
    ("activate", 1),
    ("product", 2),
    ("send", 2),
    ("spread", 0),
    ("product", 3),
    ("send", 3),
    ("spread", 1),
    ("product", 0),
    ("send", 0),
    ("product", 1),
    ("send", 1),
)


def contract_first(left, right):
    return lax.dot_general(
        left, right, (((0,), (0,)), ((), ())), preferred_element_type=jnp.float32
    )


def kernel(
    tokens_ref, wg_ref, wu_ref, wd_ref, upstream_ref,
    gt_ref, gg_ref, gu_ref, gd_ref,
    acts, weights, turned, part, part16, got1, sum1, got2, hidden, inp, inp_got, inp16, inp_all,
    in_sem, a_send, a_recv, k_send, k_recv, b1_send, b1_recv, b2_send, b2_recv,
    c1_send, c1_recv, c2_send, c2_recv, e_send, e_recv, d_send, d_recv,
):
    row, col = lax.axis_index("row"), lax.axis_index("col")
    x, y = lax.rem(row, NX), lax.div(row, NX)
    z, core = lax.div(col, 2), lax.rem(col, 2)

    def along_x(d):
        return (y * NX + lax.rem(x + d, NX), col)

    def along_y(d):
        return (lax.rem(y + d, NY) * NX + x, col)

    def along_z(d):
        return (row, lax.rem(z + d % NZ, NZ) * 2 + core)

    sibling = (row, z * 2 + 1 - core)

    halves = ((along_x, x, along_y, y), (along_y, y, along_x, x))

    def put(src, dst, send, recv, peer):
        pltpu.make_async_remote_copy(
            src, dst, send, recv, device_id=peer, device_id_type=MESH
        ).start()

    def take(ref, sem):
        pltpu.make_async_copy(ref, ref, sem).wait()

    def shard(slot, c):
        return acts.at[:, pl.ds(pl.multiple_of(slot * 2 * B + c * B, B), B), :]

    barrier = pltpu.get_barrier_semaphore()
    greet = [along_z(sign * d) for d in range(1, max(REACH) + 1) for sign in (1, -1)] + [sibling]
    greet += [along_x(d) for d in (1, 2, 3)] + [along_y(d) for d in (1, 2, 3)]
    for peer in greet:
        pl.semaphore_signal(barrier, inc=1, device_id=peer, device_id_type=MESH)
    mine = pl.ds(pl.multiple_of(core * B, B), B)
    loads = [
        pltpu.make_async_copy(tokens_ref, acts.at[0, mine, :], in_sem.at[0]),
        pltpu.make_async_copy(upstream_ref, acts.at[1, mine, :], in_sem.at[1]),
        pltpu.make_async_copy(wg_ref, weights.at[0], in_sem.at[2]),
        pltpu.make_async_copy(wu_ref, weights.at[1], in_sem.at[3]),
        pltpu.make_async_copy(wd_ref, weights.at[2], in_sem.at[4]),
    ]
    for load in loads:
        load.start()
    loads[0].wait()
    loads[1].wait()
    pl.semaphore_wait(barrier, len(greet))

    def far(s):
        return [r for r in (BASE[s + 1], -BASE[s + 1]) if r != -8]

    def near(s):
        return [sign * d for d in range(BASE[s] + 1, BASE[s + 1]) for sign in (1, -1)]

    def gather_send(s):
        for hop in range(REACH[s], 0, -1):
            for sign in (1, -1):
                have, rel = -sign * BASE[s], -sign * (BASE[s] + hop)
                if rel == 8:
                    rel = -8 if sign > 0 else 8
                if rel == 8:
                    continue
                relay = 2 * s + int(hop == REACH[s])
                put(
                    shard(SLOT[have], core), shard(SLOT[rel], core),
                    a_send.at[relay], a_recv.at[relay], along_z(sign * hop),
                )

    def to_sibling(rels, sem):
        for rel in rels:
            put(shard(SLOT[rel], core), shard(SLOT[rel], core), k_send.at[sem], k_recv.at[sem], sibling)

    def few(n):
        return acts.at[:, 0 : n * B, :]

    groups = [f(s) for s in range(STAGES) for f in (near, far)]

    def relay(s):
        take(few(len(far(s))), a_recv.at[2 * s + 1])
        if s + 1 < STAGES:
            gather_send(s + 1)
        to_sibling(far(s), 2 * s + 1)

    def nearer(s):
        if near(s):
            take(few(len(near(s))), a_recv.at[2 * s])
            to_sibling(near(s), 2 * s)

    here = []

    def project(c):
        for rel in ORDER[4 * c : 4 * c + 4]:
            group = next((g for g, rels in enumerate(groups) if rel in rels), 2 * STAGES)
            if group not in here:
                here.append(group)
                take(few(len(groups[group]) if rel else 1), k_recv.at[group])
        rows = slice(c * ROWS, (c + 1) * ROWS)
        tok, ups = acts[0, rows, :], acts[1, rows, :]
        for i in range(3):
            if i < 2:
                p = jnp.dot(tok, weights[i], preferred_element_type=jnp.float32)
            else:
                p = jnp.dot(ups, turned[2], preferred_element_type=jnp.float32)
            part[c, i] = p
            part16[c, i] = p.astype(jnp.bfloat16)
        for d in (2, 1, 3):
            for h, (first, at, _, _) in enumerate(halves):
                b = lax.rem(at + d, 4)
                block = pl.ds(pl.multiple_of(h * 64 + b * B, B), B)
                put(
                    part16.at[c, :, block, :], got1.at[c, h, d - 1], b1_send.at[c], b1_recv.at[c], first(d)
                )

    def add_first(c):
        take(got1.at[c], b1_recv.at[c])
        for h, (_, at, second, place) in enumerate(halves):
            block = pl.ds(pl.multiple_of(h * 64 + at * B, B), B)
            total = part[c, :, block, :]
            for d in range(3):
                total = total + got1[c, h, d].astype(jnp.float32)
            sum1[c, h] = total
        for d in (2, 1, 3):
            for h, (_, _, second, place) in enumerate(halves):
                j = lax.rem(place + d, 4)
                cols = pl.ds(pl.multiple_of(j * 128, 128), 128)
                put(
                    sum1.at[c, h, :, :, cols], got2.at[c, h, d - 1], b2_send.at[c], b2_recv.at[c], second(d)
                )

    def own(c, h, at, place):
        rows = pl.ds(pl.multiple_of(c * ROWS + h * 64 + at * B, B), B)
        cols = pl.ds(pl.multiple_of(place * 128, 128), 128)
        return rows, cols

    def activate(c):
        take(got2.at[c], b2_recv.at[c])
        for h, (_, at, second, place) in enumerate(halves):
            rows, cols = own(c, h, at, place)
            total = sum1[c, h, :, :, cols]
            for d in range(3):
                total = total + got2[c, h, d]
            gate, up, slope = total[0], total[1], total[2]
            s = 1.0 / (1.0 + jnp.exp(-gate))
            activated = gate * s
            hidden[0, rows, cols] = (activated * up).astype(jnp.bfloat16)
            hidden[1, rows, cols] = (slope * up * s * (1.0 + gate * (1.0 - s))).astype(jnp.bfloat16)
            hidden[2, rows, cols] = (slope * activated).astype(jnp.bfloat16)
        for d in (2, 1, 3):
            for h, (_, at, second, place) in enumerate(halves):
                rows, cols = own(c, h, at, place)
                block = hidden.at[:, rows, cols]
                put(block, block, c1_send.at[c], c1_recv.at[c], second(d))

    def spread(c):
        take(hidden.at[:, 0:96, 0:128], c1_recv.at[c])
        for d in (2, 1, 3):
            for h, (first, at, _, place) in enumerate(halves):
                rows, _ = own(c, h, at, place)
                block = hidden.at[:, rows, :]
                put(block, block, c2_send.at[c], c2_recv.at[c], first(d))

    def input_part(c):
        take(hidden.at[:, 0:96, :], c2_recv.at[c])
        rows = slice(c * ROWS, (c + 1) * ROWS)
        p = jnp.dot(hidden[1, rows, :], turned[0], preferred_element_type=jnp.float32)
        p = p + jnp.dot(hidden[2, rows, :], turned[1], preferred_element_type=jnp.float32)
        inp[c] = p.reshape(4, 2, B, 512)
        put(inp.at[c, :, 1 - core], inp_got.at[c], e_send.at[c], e_recv.at[c], sibling)

    def input_send(c):
        take(inp_got.at[c], e_recv.at[c])
        for i in reversed(range(4)):
            slot = 4 * c + i
            total = inp[c, i, core] + inp_got[c, i]
            if slot == 0:
                inp_got[c, i] = total
            else:
                inp16[c, i] = total.astype(jnp.bfloat16)
                put(inp16.at[c, i], inp_all.at[slot - 1], d_send.at[0], d_recv.at[c], along_z(ORDER[slot]))

    def weight_grads():
        pairs = ((acts, 0, hidden, 1, gg_ref), (acts, 0, hidden, 2, gu_ref), (hidden, 0, acts, 1, gd_ref))
        for left, li, right, ri, out in pairs:
            out[...] = contract_first(left[li], right[ri]).astype(jnp.bfloat16)

    gather_send(0)
    to_sibling((0,), 2 * STAGES)
    for load in loads[2:]:
        load.wait()
    for i in range(3):
        turned[i] = weights[i].T
    tasks = dict(
        relay=relay, nearer=nearer, project=project, add=add_first, activate=activate, spread=spread,
        product=input_part, send=input_send,
    )
    for name, c in SCHEDULE:
        tasks[name](c)
    weight_grads()

    for group, rels in enumerate(groups):
        if rels:
            take(few(len(rels)), a_send.at[group])
            take(few(len(rels)), k_send.at[group])
    take(few(1), k_send.at[2 * STAGES])
    for c in range(CHUNKS):
        take(got1.at[c], b1_send.at[c])
        take(got2.at[c], b2_send.at[c])
        take(hidden.at[:, 0:96, 0:128], c1_send.at[c])
        take(hidden.at[:, 0:96, :], c2_send.at[c])
        take(inp_got.at[c], e_send.at[c])

    total = inp_got[0, 0]
    for c in LAST:
        slots = range(max(4 * c, 1), 4 * c + 4)
        take(inp_all.at[slots[0] - 1 : slots[-1]], d_recv.at[c])
        for slot in slots:
            total = total + inp_all[slot - 1].astype(jnp.float32)
    gt_ref[...] = total.astype(jnp.bfloat16)
    take(inp_all, d_send.at[0])


def write_out(*refs):
    sems = refs[8]
    copies = [pltpu.make_async_copy(refs[i], refs[4 + i], sems.at[i]) for i in range(4)]
    for copy in copies:
        copy.start()
    for copy in copies:
        copy.wait()


def body(tokens, w_gate, w_up, w_down, upstream):
    bf16, f32 = jnp.bfloat16, jnp.float32
    sem = pltpu.SemaphoreType.DMA
    shapes = ((16, 512), (512, 512), (512, 512), (512, 512))
    results = pl.pallas_call(
        kernel,
        name="mlp",
        out_shape=tuple(pltpu.VMEM(shape, bf16) for shape in shapes),
        in_specs=[pl.BlockSpec(memory_space=pltpu.HBM)] * 5,
        out_specs=(pl.BlockSpec(memory_space=pltpu.VMEM),) * 4,
        scratch_shapes=[
            pltpu.VMEM((2, 512, 512), bf16),
            pltpu.VMEM((3, 512, 512), bf16),
            pltpu.VMEM((3, 512, 512), bf16),
            pltpu.VMEM((CHUNKS, 3, ROWS, 512), f32),
            pltpu.VMEM((CHUNKS, 3, ROWS, 512), bf16),
            pltpu.VMEM((CHUNKS, 2, 3, 3, B, 512), bf16),
            pltpu.VMEM((CHUNKS, 2, 3, B, 512), f32),
            pltpu.VMEM((CHUNKS, 2, 3, 3, B, 128), f32),
            pltpu.VMEM((3, 512, 512), bf16),
            pltpu.VMEM((CHUNKS, 4, 2, B, 512), f32),
            pltpu.VMEM((CHUNKS, 4, B, 512), f32),
            pltpu.VMEM((CHUNKS, 4, B, 512), bf16),
            pltpu.VMEM((15, B, 512), bf16),
            sem((5,)),
            sem((2 * STAGES,)), sem((2 * STAGES,)), sem((2 * STAGES + 1,)), sem((2 * STAGES + 1,)),
            sem((4,)), sem((4,)), sem((4,)), sem((4,)),
            sem((4,)), sem((4,)), sem((4,)), sem((4,)),
            sem((4,)), sem((4,)), sem((1,)), sem((4,)),
        ],
        compiler_params=pltpu.CompilerParams(
            collective_id=0, has_side_effects=True, vmem_limit_bytes=60 << 20
        ),
        cost_estimate=pl.CostEstimate(flops=2 << 30, bytes_accessed=4 << 20, transcendentals=0),
    )(tokens, w_gate, w_up, w_down, upstream)
    results = [pltpu.with_memory_space_constraint(r, pltpu.VMEM) for r in results]
    return pl.pallas_call(
        write_out,
        name="write_out",
        out_shape=tuple(jax.ShapeDtypeStruct(shape, bf16) for shape in shapes),
        in_specs=[pl.BlockSpec(memory_space=pltpu.VMEM)] * 4,
        out_specs=(pl.BlockSpec(memory_space=pltpu.HBM),) * 4,
        scratch_shapes=[sem((4,))],
    )(*results)


def solution(mesh):
    return jax.shard_map(
        body,
        mesh=mesh,
        in_specs=(P("col", "row"), P("row", "col"), P("row", "col"), P("col", "row"), P("col", "row")),
        out_specs=(P("col", "row"), P("row", "col"), P("row", "col"), P("col", "row")),
        check_vma=False,
    )
```

```python
import jax
import jax.numpy as jnp
from jax import lax
from jax.experimental import pallas as pl
from jax.experimental.pallas import tpu as pltpu
from jax.sharding import PartitionSpec as P

MESH = pl.DeviceIdType.MESH
NX, NY, NZ = 4, 4, 16
CHUNKS = 4
ROWS = 128
B = 16
ORDER = [0, 1, -1, 2, 3, -3, 4, -4, 5, -5, 6, -6, -2, 7, -7, 8]
SLOT = {r: s for s, r in enumerate(ORDER)}
SLOT[-8] = SLOT[8]
REACH = (3, 3, 2)
BASE = [sum(REACH[:s]) for s in range(len(REACH) + 1)]
STAGES = len(REACH)

LAST = (0, 2, 3, 1)
SCHEDULE = (
    ("relay", 0),
    ("nearer", 0),
    ("project", 0),
    ("relay", 1),
    ("nearer", 1),
    ("project", 2),
    ("relay", 2),
    ("nearer", 2),
    ("add", 0),
    ("project", 3),
    ("add", 2),
    ("project", 1),
    ("add", 3),
    ("activate", 2),
    ("activate", 0),
    ("add", 1),
    ("activate", 3),
    ("spread", 2),
    ("spread", 3),
    ("activate", 1),
    ("product", 2),
    ("send", 2),
    ("spread", 0),
    ("product", 3),
    ("send", 3),
    ("spread", 1),
    ("product", 0),
    ("send", 0),
    ("product", 1),
    ("send", 1),
)


def contract_first(left, right):
    return lax.dot_general(
        left, right, (((0,), (0,)), ((), ())), preferred_element_type=jnp.float32
    )


def kernel(
    tokens_ref, wg_ref, wu_ref, wd_ref, upstream_ref,
    gt_ref, gg_ref, gu_ref, gd_ref,
    acts, weights, turned, part, part16, got1, sum1, got2, hidden, inp, inp_got, inp16, inp_all,
    in_sem, a_send, a_recv, k_send, k_recv, b1_send, b1_recv, b2_send, b2_recv,
    c1_send, c1_recv, c2_send, c2_recv, e_send, e_recv, d_send, d_recv,
):
    row, col = lax.axis_index("row"), lax.axis_index("col")
    x, y = lax.rem(row, NX), lax.div(row, NX)
    z, core = lax.div(col, 2), lax.rem(col, 2)

    def along_x(d):
        return (y * NX + lax.rem(x + d, NX), col)

    def along_y(d):
        return (lax.rem(y + d, NY) * NX + x, col)

    def along_z(d):
        return (row, lax.rem(z + d % NZ, NZ) * 2 + core)

    sibling = (row, z * 2 + 1 - core)

    halves = ((along_x, x, along_y, y), (along_y, y, along_x, x))

    def put(src, dst, send, recv, peer):
        pltpu.make_async_remote_copy(
            src, dst, send, recv, device_id=peer, device_id_type=MESH
        ).start()

    def take(ref, sem):
        pltpu.make_async_copy(ref, ref, sem).wait()

    def shard(slot, c):
        return acts.at[:, pl.ds(pl.multiple_of(slot * 2 * B + c * B, B), B), :]

    barrier = pltpu.get_barrier_semaphore()
    greet = [along_z(sign * d) for d in range(1, max(REACH) + 1) for sign in (1, -1)] + [sibling]
    greet += [along_x(d) for d in (1, 2, 3)] + [along_y(d) for d in (1, 2, 3)]
    for peer in greet:
        pl.semaphore_signal(barrier, inc=1, device_id=peer, device_id_type=MESH)
    mine = pl.ds(pl.multiple_of(core * B, B), B)
    loads = [
        pltpu.make_async_copy(tokens_ref, acts.at[0, mine, :], in_sem.at[0]),
        pltpu.make_async_copy(upstream_ref, acts.at[1, mine, :], in_sem.at[1]),
        pltpu.make_async_copy(wg_ref, weights.at[0], in_sem.at[2]),
        pltpu.make_async_copy(wu_ref, weights.at[1], in_sem.at[3]),
        pltpu.make_async_copy(wd_ref, weights.at[2], in_sem.at[4]),
    ]
    for load in loads:
        load.start()
    loads[0].wait()
    loads[1].wait()
    pl.semaphore_wait(barrier, len(greet))

    def far(s):
        return [r for r in (BASE[s + 1], -BASE[s + 1]) if r != -8]

    def near(s):
        return [sign * d for d in range(BASE[s] + 1, BASE[s + 1]) for sign in (1, -1)]

    def gather_send(s):
        for hop in range(REACH[s], 0, -1):
            for sign in (1, -1):
                have, rel = -sign * BASE[s], -sign * (BASE[s] + hop)
                if rel == 8:
                    rel = -8 if sign > 0 else 8
                if rel == 8:
                    continue
                relay = 2 * s + int(hop == REACH[s])
                put(
                    shard(SLOT[have], core), shard(SLOT[rel], core),
                    a_send.at[relay], a_recv.at[relay], along_z(sign * hop),
                )

    def to_sibling(rels, sem):
        for rel in rels:
            put(shard(SLOT[rel], core), shard(SLOT[rel], core), k_send.at[sem], k_recv.at[sem], sibling)

    def few(n):
        return acts.at[:, 0 : n * B, :]

    groups = [f(s) for s in range(STAGES) for f in (near, far)]

    def relay(s):
        take(few(len(far(s))), a_recv.at[2 * s + 1])
        if s + 1 < STAGES:
            gather_send(s + 1)
        to_sibling(far(s), 2 * s + 1)

    def nearer(s):
        if near(s):
            take(few(len(near(s))), a_recv.at[2 * s])
            to_sibling(near(s), 2 * s)

    here = []

    def project(c):
        for rel in ORDER[4 * c : 4 * c + 4]:
            group = next((g for g, rels in enumerate(groups) if rel in rels), 2 * STAGES)
            if group not in here:
                here.append(group)
                take(few(len(groups[group]) if rel else 1), k_recv.at[group])
        rows = slice(c * ROWS, (c + 1) * ROWS)
        tok, ups = acts[0, rows, :], acts[1, rows, :]
        for i in range(3):
            if i < 2:
                p = jnp.dot(tok, weights[i], preferred_element_type=jnp.float32)
            else:
                p = jnp.dot(ups, turned[2], preferred_element_type=jnp.float32)
            part[c, i] = p
            part16[c, i] = p.astype(jnp.bfloat16)
        for d in (2, 1, 3):
            for h, (first, at, _, _) in enumerate(halves):
                b = lax.rem(at + d, 4)
                block = pl.ds(pl.multiple_of(h * 64 + b * B, B), B)
                put(
                    part16.at[c, :, block, :], got1.at[c, h, d - 1], b1_send.at[c], b1_recv.at[c], first(d)
                )

    def add_first(c):
        take(got1.at[c], b1_recv.at[c])
        for h, (_, at, second, place) in enumerate(halves):
            block = pl.ds(pl.multiple_of(h * 64 + at * B, B), B)
            total = part[c, :, block, :]
            for d in range(3):
                total = total + got1[c, h, d].astype(jnp.float32)
            sum1[c, h] = total
        for d in (2, 1, 3):
            for h, (_, _, second, place) in enumerate(halves):
                j = lax.rem(place + d, 4)
                cols = pl.ds(pl.multiple_of(j * 128, 128), 128)
                put(
                    sum1.at[c, h, :, :, cols], got2.at[c, h, d - 1], b2_send.at[c], b2_recv.at[c], second(d)
                )

    def own(c, h, at, place):
        rows = pl.ds(pl.multiple_of(c * ROWS + h * 64 + at * B, B), B)
        cols = pl.ds(pl.multiple_of(place * 128, 128), 128)
        return rows, cols

    def activate(c):
        take(got2.at[c], b2_recv.at[c])
        for h, (_, at, second, place) in enumerate(halves):
            rows, cols = own(c, h, at, place)
            total = sum1[c, h, :, :, cols]
            for d in range(3):
                total = total + got2[c, h, d]
            gate, up, slope = total[0], total[1], total[2]
            s = 1.0 / (1.0 + jnp.exp(-gate))
            activated = gate * s
            hidden[0, rows, cols] = (activated * up).astype(jnp.bfloat16)
            hidden[1, rows, cols] = (slope * up * s * (1.0 + gate * (1.0 - s))).astype(jnp.bfloat16)
            hidden[2, rows, cols] = (slope * activated).astype(jnp.bfloat16)
        for d in (2, 1, 3):
            for h, (_, at, second, place) in enumerate(halves):
                rows, cols = own(c, h, at, place)
                block = hidden.at[:, rows, cols]
                put(block, block, c1_send.at[c], c1_recv.at[c], second(d))

    def spread(c):
        take(hidden.at[:, 0:96, 0:128], c1_recv.at[c])
        for d in (2, 1, 3):
            for h, (first, at, _, place) in enumerate(halves):
                rows, _ = own(c, h, at, place)
                block = hidden.at[:, rows, :]
                put(block, block, c2_send.at[c], c2_recv.at[c], first(d))

    def input_part(c):
        take(hidden.at[:, 0:96, :], c2_recv.at[c])
        rows = slice(c * ROWS, (c + 1) * ROWS)
        p = jnp.dot(hidden[1, rows, :], turned[0], preferred_element_type=jnp.float32)
        p = p + jnp.dot(hidden[2, rows, :], turned[1], preferred_element_type=jnp.float32)
        inp[c] = p.reshape(4, 2, B, 512)
        put(inp.at[c, :, 1 - core], inp_got.at[c], e_send.at[c], e_recv.at[c], sibling)

    def input_send(c):
        take(inp_got.at[c], e_recv.at[c])
        for i in reversed(range(4)):
            slot = 4 * c + i
            total = inp[c, i, core] + inp_got[c, i]
            if slot == 0:
                inp_got[c, i] = total
            else:
                inp16[c, i] = total.astype(jnp.bfloat16)
                put(inp16.at[c, i], inp_all.at[slot - 1], d_send.at[0], d_recv.at[c], along_z(ORDER[slot]))

    def weight_grads():
        pairs = ((acts, 0, hidden, 1, gg_ref), (acts, 0, hidden, 2, gu_ref), (hidden, 0, acts, 1, gd_ref))
        for left, li, right, ri, out in pairs:
            out[...] = contract_first(left[li], right[ri]).astype(jnp.bfloat16)

    gather_send(0)
    to_sibling((0,), 2 * STAGES)
    for load in loads[2:]:
        load.wait()
    for i in range(3):
        turned[i] = weights[i].T
    tasks = dict(
        relay=relay, nearer=nearer, project=project, add=add_first, activate=activate, spread=spread,
        product=input_part, send=input_send,
    )
    for name, c in SCHEDULE:
        tasks[name](c)
    weight_grads()

    for group, rels in enumerate(groups):
        if rels:
            take(few(len(rels)), a_send.at[group])
            take(few(len(rels)), k_send.at[group])
    take(few(1), k_send.at[2 * STAGES])
    for c in range(CHUNKS):
        take(got1.at[c], b1_send.at[c])
        take(got2.at[c], b2_send.at[c])
        take(hidden.at[:, 0:96, 0:128], c1_send.at[c])
        take(hidden.at[:, 0:96, :], c2_send.at[c])
        take(inp_got.at[c], e_send.at[c])

    total = inp_got[0, 0]
    for c in LAST:
        slots = range(max(4 * c, 1), 4 * c + 4)
        take(inp_all.at[slots[0] - 1 : slots[-1]], d_recv.at[c])
        for slot in slots:
            total = total + inp_all[slot - 1].astype(jnp.float32)
    gt_ref[...] = total.astype(jnp.bfloat16)
    take(inp_all, d_send.at[0])


def write_out(*refs):
    sems = refs[8]
    copies = [pltpu.make_async_copy(refs[i], refs[4 + i], sems.at[i]) for i in range(4)]
    for copy in copies:
        copy.start()
    for copy in copies:
        copy.wait()


def body(tokens, w_gate, w_up, w_down, upstream):
    bf16, f32 = jnp.bfloat16, jnp.float32
    sem = pltpu.SemaphoreType.DMA
    shapes = ((16, 512), (512, 512), (512, 512), (512, 512))
    results = pl.pallas_call(
        kernel,
        name="mlp",
        out_shape=tuple(pltpu.VMEM(shape, bf16) for shape in shapes),
        in_specs=[pl.BlockSpec(memory_space=pltpu.HBM)] * 5,
        out_specs=(pl.BlockSpec(memory_space=pltpu.VMEM),) * 4,
        scratch_shapes=[
            pltpu.VMEM((2, 512, 512), bf16),
            pltpu.VMEM((3, 512, 512), bf16),
            pltpu.VMEM((3, 512, 512), bf16),
            pltpu.VMEM((CHUNKS, 3, ROWS, 512), f32),
            pltpu.VMEM((CHUNKS, 3, ROWS, 512), bf16),
            pltpu.VMEM((CHUNKS, 2, 3, 3, B, 512), bf16),
            pltpu.VMEM((CHUNKS, 2, 3, B, 512), f32),
            pltpu.VMEM((CHUNKS, 2, 3, 3, B, 128), f32),
            pltpu.VMEM((3, 512, 512), bf16),
            pltpu.VMEM((CHUNKS, 4, 2, B, 512), f32),
            pltpu.VMEM((CHUNKS, 4, B, 512), f32),
            pltpu.VMEM((CHUNKS, 4, B, 512), bf16),
            pltpu.VMEM((15, B, 512), bf16),
            sem((5,)),
            sem((2 * STAGES,)), sem((2 * STAGES,)), sem((2 * STAGES + 1,)), sem((2 * STAGES + 1,)),
            sem((4,)), sem((4,)), sem((4,)), sem((4,)),
            sem((4,)), sem((4,)), sem((4,)), sem((4,)),
            sem((4,)), sem((4,)), sem((1,)), sem((4,)),
        ],
        compiler_params=pltpu.CompilerParams(
            collective_id=0, has_side_effects=True, vmem_limit_bytes=60 << 20
        ),
        cost_estimate=pl.CostEstimate(flops=2 << 30, bytes_accessed=4 << 20, transcendentals=0),
    )(tokens, w_gate, w_up, w_down, upstream)
    results = [pltpu.with_memory_space_constraint(r, pltpu.VMEM) for r in results]
    return pl.pallas_call(
        write_out,
        name="write_out",
        out_shape=tuple(jax.ShapeDtypeStruct(shape, bf16) for shape in shapes),
        in_specs=[pl.BlockSpec(memory_space=pltpu.VMEM)] * 4,
        out_specs=(pl.BlockSpec(memory_space=pltpu.HBM),) * 4,
        scratch_shapes=[sem((4,))],
    )(*results)


def solution(mesh):
    return jax.shard_map(
        body,
        mesh=mesh,
        in_specs=(P("col", "row"), P("row", "col"), P("row", "col"), P("col", "row"), P("col", "row")),
        out_specs=(P("col", "row"), P("row", "col"), P("row", "col"), P("col", "row")),
        check_vma=False,
    )
```
